512 devices in a mesh: inner: 32 (over y_hi, x, core), outer: 16 (over z, y_lo).
Axes of the slice: x: 4, y: 8 (y_hi: 4, y_lo: 2; y = y_hi * 2 + y_lo), z: 8, core: 2. Of those that a mesh axis runs over, the one named last changes fastest.
Arguments:
- query: bfloat16 [196608, 512], P(('inner', 'outer')), may hold values from -6 to 6
- keys: bfloat16 [196608, 512], P(('inner', 'outer')), may hold values from -6 to 6
- values: bfloat16 [196608, 512], P(('inner', 'outer')), may hold values from -6 to 6
- output: bfloat16 [196608, 512], P(('inner', 'outer')), may hold values from -4 to 4
- grad_output: bfloat16 [196608, 512], P(('inner', 'outer')), may hold values from -6 to 6
- log_sum_exp: float32 [8, 196608], P(None, ('inner', 'outer')), may hold values from 4 to 6
- order: int32 [512, 384], P(('inner', 'outer')), may hold values from 0 to 383, each once within a row
- layout: int32 [512, 3], P(('inner', 'outer')), may hold values 0 or 1
Outputs:
- grad_query: bfloat16 [196608, 512], P(('inner', 'outer'))
- grad_keys: bfloat16 [196608, 512], P(('inner', 'outer'))
- grad_values: bfloat16 [196608, 512], P(('inner', 'outer'))
The draws below stay inside these ranges and needn't reach their ends.
Inputs may be any that keep to these rules, and one draw needn't show every extreme that they name: `order`: each row is a permutation of 0 to 383. `layout`: entries [b, d - 1] with b < d are ignored.
All inputs are finite; a program needn't handle non-finite values. No bound on the sum of `layout` on one device may be relied on, other than what follows from the above.
Results may differ from the reference program's by a relative error of at most 0.0049.
Values may be sent and summed in bfloat16 or wider, within the bound.
No kernel may reach another device: no remote copies, remote signals or barrier semaphores. Data moves between devices by JAX's collectives and lax.ppermute only.
A program may use at most 64 MiB of HBM per device.

```python
import jax
import jax.numpy as jnp
from jax import lax

H = 8
HD = 64
WIN = 3
TOK_DEV = 384
BLOCKS = 512
TOKENS = 196608
C = 512


def set_ends(entries, own_key, low, largest):
    shape = entries.shape
    place = [jax.random.randint(jax.random.fold_in(own_key, axis), (), 0, shape[axis]) for axis in range(len(shape))]
    entries = entries.at[tuple(place)].set(low)
    longest = shape.index(max(shape))
    place[longest] = (place[longest] + 1) % shape[longest]
    return entries.at[tuple(place)].set(largest)


def steps_of(own_key, extent, split, low, high):
    def one(dim, blocks):
        heights = jax.random.uniform(jax.random.fold_in(jax.random.fold_in(own_key, 6), dim), (blocks,), jnp.float32, low / len(split), high / len(split))
        return jnp.repeat(jnp.exp(heights), extent[dim] // blocks).reshape((-1,) + (1,) * (len(extent) - dim - 1))

    level = one(*split[0])
    for cut in split[1:]:
        level = level * one(*cut)
    return level


def centred(own_key, extent, scale, most, pieces=(), kind=jnp.bfloat16):
    values = jax.random.normal(own_key, extent, jnp.float32) * scale
    if len(pieces) > 0:
        values = steps_of(own_key, extent, pieces, -0.22, 0.18) * values
    return jnp.clip(values, min=-most, max=most).astype(kind)


def setup_inputs(seed: int = 0) -> dict:
    splits = jax.random.split(jax.random.key(seed), 9)
    return {
        "query": centred(splits[0], (TOKENS, C), 1.0, 6.0, ((0, 512),)),
        "keys": centred(splits[1], (TOKENS, C), 1.0, 6.0, ((0, 512),)),
        "values": centred(splits[2], (TOKENS, C), 1.0, 6.0, ((0, 512),)),
        "output": centred(splits[3], (TOKENS, C), 0.5, 4.0, ((0, 512),)),
        "grad_output": centred(splits[4], (TOKENS, C), 1.0, 6.0, ((0, 512),)),
        "log_sum_exp": jnp.clip(4.0 + 2.0 * jax.random.uniform(splits[5], (H, TOKENS), jnp.float32) ** steps_of(splits[5], (H, TOKENS), ((1, 512),), -0.2, 0.2), 4.0, 6.0),
        "order": jax.vmap(lambda own: jax.random.permutation(own, TOK_DEV))(jax.random.split(splits[6], BLOCKS)).reshape((BLOCKS, TOK_DEV)).astype(jnp.int32),
        "layout": set_ends((jax.random.randint(splits[7], (BLOCKS, WIN), 0, 2) < 1).astype(jnp.int32), jax.random.fold_in(splits[7], 1), 0, 1),
    }


SCALE = 0.125


def tile_grads(query, keys, values, dout, lse, delta, visible):
    qf = query.astype(jnp.float32)
    kf = keys.astype(jnp.float32)
    vf = values.astype(jnp.float32)
    df = dout.astype(jnp.float32)
    scores = jnp.einsum('qhd,khd->hqk', qf, kf) * SCALE
    probs = jnp.where(visible, jnp.exp(scores - lse[:, :, None]), jnp.float32(0.0))
    probs_low = probs.astype(jnp.bfloat16).astype(jnp.float32)
    dprobs = jnp.einsum('qhd,khd->hqk', df, vf)
    dscores = (probs * (dprobs - delta[:, :, None])).astype(jnp.bfloat16).astype(jnp.float32)
    grad_v = jnp.einsum('hqk,qhd->khd', probs_low, df)
    grad_q = SCALE * jnp.einsum('hqk,khd->qhd', dscores, kf)
    grad_k = SCALE * jnp.einsum('hqk,qhd->khd', dscores, qf)
    return grad_q, grad_k, grad_v


def reference(query, keys, values, output, grad_output, log_sum_exp, order, layout):
    nblocks = TOKENS // TOK_DEV
    shape = (nblocks, TOK_DEV, H, HD)
    qb = query.reshape(shape)
    kb = keys.reshape(shape)
    vb = values.reshape(shape)
    ob = output.reshape(shape)
    db = grad_output.reshape(shape)
    lse_blocks = jnp.transpose(log_sum_exp.reshape(H, nblocks, TOK_DEV), (1, 0, 2))

    def step(carry, block):
        acc_k, acc_v = carry
        q = qb[block]
        dout = db[block]
        lse = lse_blocks[block]
        delta = jnp.sum(dout.astype(jnp.float32) * ob[block].astype(jnp.float32), axis=2).T
        rank = order[block]
        grad_q = jnp.zeros((TOK_DEV, H, HD), jnp.float32)
        for dist in range(WIN + 1):
            source = jnp.maximum(block - dist, 0).astype(jnp.int32)
            if dist == 0:
                visible = (rank[:, None] >= rank[None, :])[None]
            else:
                visible = jnp.logical_and(layout[block, dist - 1] > 0, block >= dist)
            part_q, part_k, part_v = tile_grads(q, kb[source], vb[source], dout, lse, delta, visible)
            grad_q = grad_q + part_q
            acc_k = acc_k.at[source].add(part_k)
            acc_v = acc_v.at[source].add(part_v)
        return (acc_k, acc_v), grad_q.astype(jnp.bfloat16)

    zeros = jnp.zeros(shape, jnp.float32)
    (acc_k, acc_v), grad_q = lax.scan(step, (zeros, zeros), jnp.arange(nblocks, dtype=jnp.int32))
    flat = (TOKENS, H * HD)
    return (grad_q.reshape(flat), acc_k.astype(jnp.bfloat16).reshape(flat), acc_v.astype(jnp.bfloat16).reshape(flat))
```

```python
import functools
import math

import jax
import jax.numpy as jnp
from jax import lax
from jax.experimental import pallas as pl
from jax.experimental.pallas import tpu as pltpu
from jax.sharding import PartitionSpec as P

AXES = ("inner", "outer")
HEADS = 8
SIZE = 64
PAIR = 2 * SIZE
CHUNKS = 2
DIRECT = False
COST = 8
HC = HEADS // CHUNKS
WC = HC * SIZE
EXP_SCALE = 0.125 / math.log(2.0)
HIDDEN = -1e30
f32 = jnp.float32
bf16 = jnp.bfloat16

VIS = 48


def dot(a, b, ca, cb):
    return lax.dot_general(a, b, (((ca,), (cb,)), ((), ())), preferred_element_type=f32)


def pieces(x):
    a = x.astype(bf16)
    r = x - a.astype(f32)
    b = r.astype(bf16)
    c = (r - b.astype(f32)).astype(bf16)
    return a, b, c


def pack_kernel(blk, layout, lse, *refs):
    far, outs, near, sems = refs[:5], refs[5 : 5 + 2 * CHUNKS], refs[-6:-1], refs[-1]
    copies = [pltpu.make_async_copy(far[i], near[i], sems.at[i]) for i in range(5)]
    for copy in copies:
        copy.start()
    for copy in copies:
        copy.wait()
    q, k, v, o, do = near
    rows = q.shape[0]
    qs, ks = outs[:CHUNKS], outs[CHUNKS:]
    for c in range(CHUNKS):
        w = slice(c * WC, (c + 1) * WC)
        ks[c][:, :WC] = k[:, w]
        ks[c][:, WC:] = v[:, w]
        qs[c][:, :WC] = q[:, w]
        qs[c][:, WC : 2 * WC] = do[:, w]
    lane = lax.broadcasted_iota(jnp.int32, (1, 128), 1)
    prod = do[...].astype(f32) * o[...].astype(f32)
    hi = prod.astype(bf16)
    lo = (prod - hi.astype(f32)).astype(bf16)
    feat = lax.broadcasted_iota(jnp.int32, (HEADS * SIZE, 128), 0) // SIZE
    flane = lax.broadcasted_iota(jnp.int32, (HEADS * SIZE, 128), 1)
    pick = jnp.where((flane % 8 == feat) & (flane >= 24) & (flane < 48), 1.0, 0.0).astype(bf16)
    delta = dot(hi, pick, 1, 0) + dot(lo, pick, 1, 0)
    d1, d2, d3 = (x.astype(f32) for x in pieces(delta))
    dpart = jnp.where(lane < 32, d1, jnp.where(lane < 40, d2, d3))
    l1, l2, l3 = (x.astype(f32) for x in pieces(lse[...] * 8.0))
    stack = jnp.concatenate([l1, l2, l3, jnp.zeros_like(l1)], 0).astype(bf16)
    r = lax.broadcasted_iota(jnp.int32, (32, 128), 0)
    c = lax.broadcasted_iota(jnp.int32, (32, 128), 1)
    eye = jnp.where((r == c) & (r < 24), 1.0, 0.0).astype(bf16)
    lpart = dot(stack, eye, 0, 0)
    vis = jnp.zeros((1, 128), f32)
    for d in (1, 2, 3):
        seen = jnp.logical_and(layout[0, d - 1] > 0, blk[0] >= d)
        vis = jnp.where((lane == VIS + d - 1) & jnp.logical_not(seen), f32(HIDDEN), vis)
    aux = jnp.where(lane < 24, lpart, jnp.where(lane < 48, dpart, jnp.broadcast_to(vis, (rows, 128))))
    qs[0][:, 2 * WC :] = aux.astype(bf16)


def tile(q, aux, kv, c, hp, dist, rank_row=None, rank_col=None):
    at = pl.ds(pl.multiple_of(hp * PAIR, PAIR), PAIR)
    at2 = pl.ds(pl.multiple_of(WC + hp * PAIR, PAIR), PAIR)
    qp, dop, kp, vp = q[:, at], q[:, at2], kv[:, at], kv[:, at2]
    lane = lax.broadcasted_iota(jnp.int32, (1, PAIR), 1)
    half = lax.broadcasted_iota(jnp.int32, qp.shape, 1) // SIZE
    qa = jnp.concatenate([qp, aux], 1)
    da = jnp.concatenate([dop, aux], 1)
    km, qm, dm, pb, db = [], [], [], [], []
    for h in range(2):
        head = c * HC + hp * 2 + h
        sel = jnp.where((lane % 8 == head) & (lane < 24), -1.0, 0.0)
        if dist is not None:
            sel = jnp.where(lane == VIS - 1 + dist, 1.0, sel)
        sel_d = jnp.where((lane % 8 == head) & (lane >= 24) & (lane < 48), -1.0, 0.0)
        mine = half == h
        zero = jnp.zeros_like(kp)
        km.append(jnp.where(mine, kp, zero))
        vm = jnp.where(mine, vp, zero)
        qm.append(jnp.where(mine, qp, zero))
        dm.append(jnp.where(mine, dop, zero))
        s = dot(jnp.concatenate([km[h], jnp.broadcast_to(sel, kp.shape).astype(bf16)], 1), qa, 1, 1)
        dp = dot(jnp.concatenate([vm, jnp.broadcast_to(sel_d, kp.shape).astype(bf16)], 1), da, 1, 1)
        p = jnp.exp2(s * EXP_SCALE)
        if rank_row is not None:
            p = jnp.where(rank_row >= rank_col, p, 0.0)
        pb.append(p.astype(bf16))
        db.append((p * dp).astype(bf16))
    dv = dot(jnp.concatenate(pb, 1), jnp.concatenate(dm, 0), 1, 0)
    dk = dot(jnp.concatenate(db, 1), jnp.concatenate(qm, 0), 1, 0)
    dq = dot(jnp.concatenate(db, 0), jnp.concatenate(km, 0), 0, 0)
    return dq, dk, dv


def pairs(body):
    def step(hp, _):
        body(hp, pl.ds(pl.multiple_of(hp * PAIR, PAIR), PAIR), pl.ds(pl.multiple_of(WC + hp * PAIR, PAIR), PAIR))
        return 0

    lax.fori_loop(0, HC // 2, step, 0)


def diag_kernel(c, q, aux, kv, rank_row, rank_col, dq, dkv):
    def body(hp, at, at2):
        x, y, z = tile(q, aux[...], kv, c, hp, None, rank_row[...], rank_col[...])
        dq[:, at] = x
        dkv[:, at] = y
        dkv[:, at2] = z

    pairs(body)


def cross_kernel(c, odd, q0, a0, q1, a1, k0, k1, dq, dkv, *refs):
    before, (dq_out, dkv_out, dq1, dkv1) = refs[:-4], refs[-4:]
    near = jnp.where(odd[0] == 0, 3, 1)
    base = 0
    for part in before:
        dq1[:, base : base + WC] = part[...]
        base += WC

    def body(hp, at, at2):
        x, y, z = tile(q0, a0[...], k1, c, hp, 2)
        dq_out[:, at] = dq[:, at] + x
        x, y2, z2 = tile(q1, a1[...], k1, c, hp, near)
        dkv1[:, at] = y + y2
        dkv1[:, at2] = z + z2
        to = pl.ds(pl.multiple_of(base + hp * PAIR, PAIR), PAIR)

        @pl.when(odd[0] == 0)
        def _():
            x3, y3, z3 = tile(q1, a1[...], k0, c, hp, 1)
            dq1[:, to] = ((x + x3) * 0.125).astype(bf16)
            dkv_out[:, at] = dkv[:, at] + y3
            dkv_out[:, at2] = dkv[:, at2] + z3

        @pl.when(odd[0] != 0)
        def _():
            dq1[:, to] = (x * 0.125).astype(bf16)
            dkv_out[:, at] = dkv[:, at]
            dkv_out[:, at2] = dkv[:, at2]

    pairs(body)


def last_kernel(c, odd, q2, a2, k1, dkv1, *refs):
    before, (dq2, out) = refs[:-2], refs[-2:]
    base = 0
    for part in before:
        dq2[:, base : base + WC] = part[...]
        base += WC

    def body(hp, at, at2):
        to = pl.ds(pl.multiple_of(base + hp * PAIR, PAIR), PAIR)

        @pl.when(odd[0] != 0)
        def _():
            x, y, z = tile(q2, a2[...], k1, c, hp, 3)
            dq2[:, to] = (x * 0.125).astype(bf16)
            out[:, at] = ((dkv1[:, at] + y) * 0.125).astype(bf16)
            out[:, at2] = (dkv1[:, at2] + z).astype(bf16)

        @pl.when(odd[0] == 0)
        def _():
            dq2[:, to] = jnp.zeros((dq2.shape[0], PAIR), bf16)
            out[:, at] = (dkv1[:, at] * 0.125).astype(bf16)
            out[:, at2] = dkv1[:, at2].astype(bf16)

    pairs(body)


def sum_kernel(*refs):
    dqs, dkvs, backs, (r1, r2, gq, gk, gv) = refs[:CHUNKS], refs[CHUNKS : 2 * CHUNKS], refs[2 * CHUNKS : 3 * CHUNKS], refs[3 * CHUNKS :]
    for c in range(CHUNKS):
        w = slice(c * WC, (c + 1) * WC)
        gq[:, w] = (dqs[c][...] * 0.125 + r1[:, w].astype(f32) + r2[:, w].astype(f32)).astype(bf16)
        gk[:, w] = (dkvs[c][:, :WC] * 0.125 + backs[c][:, :WC].astype(f32)).astype(bf16)
        gv[:, w] = (dkvs[c][:, WC:] + backs[c][:, WC:].astype(f32)).astype(bf16)


VM = pl.BlockSpec(memory_space=pltpu.VMEM)
SM = pl.BlockSpec(memory_space=pltpu.SMEM)


def call(kernel, outs, n_smem, args, scratch=(), flops=0, n_far=0):
    near = len(args) - n_smem - n_far
    return pl.pallas_call(
        kernel,
        out_shape=outs,
        in_specs=[SM] * n_smem + [VM] * near + [pl.BlockSpec(memory_space=pltpu.HBM)] * n_far,
        out_specs=[VM] * len(outs),
        scratch_shapes=list(scratch),
        cost_estimate=pl.CostEstimate(flops=flops, bytes_accessed=4 << 20, transcendentals=0),
        compiler_params=pltpu.CompilerParams(vmem_limit_bytes=16 << 20),
    )(*args)


def per_device(query, keys, values, output, grad_output, log_sum_exp, order, layout):
    rows = query.shape[0]
    n = lax.axis_size(AXES)
    block = lax.axis_index(AXES)
    blk = jnp.reshape(block, (1,)).astype(jnp.int32)
    odd = blk % 2

    def arr(cols, kind):
        return jax.ShapeDtypeStruct((rows, cols), kind)

    def shifted(x, by, keep=lambda i: True):
        return lax.ppermute(x, AXES, [(i - by, i) for i in range(n) if 0 <= i - by < n and keep(i)])

    def swapped(x):
        return lax.ppermute(x, AXES, [(i ^ 1, i) for i in range(n)])

    tile_flops = COST * 5 * 2 * rows * rows * SIZE * HEADS
    qw = [2 * WC + (128 if c == 0 else 0) for c in range(CHUNKS)]
    packed = call(
        pack_kernel,
        [arr(w, bf16) for w in qw] + [arr(2 * WC, bf16)] * CHUNKS,
        2,
        (blk, layout, log_sum_exp, query, keys, values, output, grad_output),
        scratch=[pltpu.VMEM((rows, HEADS * SIZE), bf16)] * 5 + [pltpu.SemaphoreType.DMA((5,))],
        flops=1 << 20,
        n_far=5,
    )
    q0, k0 = packed[:CHUNKS], packed[CHUNKS:]
    k1, q1 = [], []
    for c in range(CHUNKS):
        q1.append(swapped(q0[c]))
        k1.append(shifted(k0[c], 2))
    q2 = [shifted(q1[c], -2, lambda i: i % 2 == 1) for c in range(CHUNKS)]
    if DIRECT:
        q2[-1] = lax.ppermute(q0[-1], AXES, [(i + 1, i) for i in range(1, n - 1, 2)])
    rank_row, rank_col = order, jnp.reshape(order, (rows, 1))
    a0, a1, a2 = (x[0][:, 2 * WC :] for x in (q0, q1, q2))
    dqs, dkvs, back_kv, dq1, dq2 = [], [], [], (), ()
    for c in range(CHUNKS):
        dq, dkv = call(
            functools.partial(diag_kernel, c),
            [arr(WC, f32), arr(2 * WC, f32)],
            0,
            (q0[c], a0, k0[c], rank_row, rank_col),
            flops=tile_flops // CHUNKS,
        )
        dq, dkv, x, dkv1 = call(
            functools.partial(cross_kernel, c),
            [arr(WC, f32), arr(2 * WC, f32), arr((c + 1) * WC, bf16), arr(2 * WC, f32)],
            1,
            (odd, q0[c], a0, q1[c], a1, k0[c], k1[c], dq, dkv, *dq1),
            flops=3 * tile_flops // CHUNKS,
        )
        dq1 = (x,)
        dqs.append(dq)
        dkvs.append(dkv)
        x, send = call(
            functools.partial(last_kernel, c),
            [arr((c + 1) * WC, bf16), arr(2 * WC, bf16)],
            1,
            (odd, q2[c], a2, k1[c], dkv1, *dq2),
            flops=tile_flops // CHUNKS,
        )
        dq2 = (x,)
        back_kv.append(shifted(send, -2))
    back_q1 = swapped(dq1[0])
    back_q2 = lax.ppermute(dq2[0], AXES, [(i, i + 1) for i in range(1, n - 1, 2)])
    return tuple(
        call(sum_kernel, [arr(HEADS * SIZE, bf16)] * 3, 0, (*dqs, *dkvs, *back_kv, back_q1, back_q2), flops=1 << 20)
    )


def solution(mesh):
    rows = P(AXES, None)
    return jax.shard_map(
        per_device,
        mesh=mesh,
        in_specs=(rows, rows, rows, rows, rows, P(None, AXES), rows, rows),
        out_specs=(rows, rows, rows),
        check_vma=False,
    )
```

```python
import functools
import math

import jax
import jax.numpy as jnp
from jax import lax
from jax.experimental import pallas as pl
from jax.experimental.pallas import tpu as pltpu
from jax.sharding import PartitionSpec as P

AXES = ("inner", "outer")
HEADS = 8
SIZE = 64
PAIR = 2 * SIZE
CHUNKS = 2
COST = 8
SPAN = 128
HC = HEADS // CHUNKS
WC = HC * SIZE
EXP_SCALE = 0.125 / math.log(2.0)
HIDDEN = -1e30
f32 = jnp.float32
bf16 = jnp.bfloat16

VIS = 48


def dot(a, b, ca, cb):
    return lax.dot_general(a, b, (((ca,), (cb,)), ((), ())), preferred_element_type=f32)


def pieces(x):
    a = x.astype(bf16)
    r = x - a.astype(f32)
    b = r.astype(bf16)
    c = (r - b.astype(f32)).astype(bf16)
    return a, b, c


def pack_q(blk, layout, lse, order, everything, *outs):
    q, do, o = (everything.at[:, i * HEADS * SIZE : (i + 1) * HEADS * SIZE] for i in range(3))
    qs, rank = outs[:CHUNKS], outs[CHUNKS]
    rows = q.shape[0]
    for c in range(CHUNKS):
        w = slice(c * WC, (c + 1) * WC)
        qs[c][:, :WC] = q[:, w]
        qs[c][:, WC : 2 * WC] = do[:, w]
    lane = lax.broadcasted_iota(jnp.int32, (1, 128), 1)
    prod = do[...].astype(f32) * o[...].astype(f32)
    hi = prod.astype(bf16)
    lo = (prod - hi.astype(f32)).astype(bf16)
    feat = lax.broadcasted_iota(jnp.int32, (HEADS * SIZE, 128), 0) // SIZE
    flane = lax.broadcasted_iota(jnp.int32, (HEADS * SIZE, 128), 1)
    pick = jnp.where((flane % 8 == feat) & (flane >= 24) & (flane < 48), 1.0, 0.0).astype(bf16)
    delta = dot(hi, pick, 1, 0) + dot(lo, pick, 1, 0)
    d1, d2, d3 = (x.astype(f32) for x in pieces(delta))
    dpart = jnp.where(lane < 32, d1, jnp.where(lane < 40, d2, d3))
    l1, l2, l3 = (x.astype(f32) for x in pieces(lse[...] * 8.0))
    stack = jnp.concatenate([l1, l2, l3, jnp.zeros_like(l1)], 0).astype(bf16)
    r = lax.broadcasted_iota(jnp.int32, (32, 128), 0)
    c = lax.broadcasted_iota(jnp.int32, (32, 128), 1)
    eye = jnp.where((r == c) & (r < 24), 1.0, 0.0).astype(bf16)
    lpart = dot(stack, eye, 0, 0)
    vis = jnp.zeros((1, 128), f32)
    for d in (1, 2, 3):
        seen = jnp.logical_and(layout[0, d - 1] > 0, blk[0] >= d)
        vis = jnp.where((lane == VIS + d - 1) & jnp.logical_not(seen), f32(HIDDEN), vis)
    aux = jnp.where(lane < 24, lpart, jnp.where(lane < 48, dpart, jnp.broadcast_to(vis, (rows, 128))))
    qs[0][:, 2 * WC :] = aux.astype(bf16)
    rank[...] = jnp.broadcast_to(order[...].astype(f32), rank.shape)


def tile(q, aux, kv, c, hp, dist, rank_row=None, rank_col=None):
    at = pl.ds(pl.multiple_of(hp * PAIR, PAIR), PAIR)
    at2 = pl.ds(pl.multiple_of(WC + hp * PAIR, PAIR), PAIR)
    at_k = pl.ds(pl.multiple_of(c * WC + hp * PAIR, PAIR), PAIR)
    at_v = pl.ds(pl.multiple_of((CHUNKS + c) * WC + hp * PAIR, PAIR), PAIR)
    qp, dop, kp, vp = q[:, at], q[:, at2], kv[:, at_k], kv[:, at_v]
    lane = lax.broadcasted_iota(jnp.int32, (1, PAIR), 1)
    half = lax.broadcasted_iota(jnp.int32, qp.shape, 1) // SIZE
    qa = jnp.concatenate([qp, aux], 1)
    da = jnp.concatenate([dop, aux], 1)
    km, qm, dm, pb, db = [], [], [], [], []
    for h in range(2):
        head = c * HC + hp * 2 + h
        sel = jnp.where((lane % 8 == head) & (lane < 24), -1.0, 0.0)
        if dist is not None:
            sel = jnp.where(lane == VIS - 1 + dist, 1.0, sel)
        sel_d = jnp.where((lane % 8 == head) & (lane >= 24) & (lane < 48), -1.0, 0.0)
        mine = half == h
        zero = jnp.zeros_like(kp)
        km.append(jnp.where(mine, kp, zero))
        vm = jnp.where(mine, vp, zero)
        qm.append(jnp.where(mine, qp, zero))
        dm.append(jnp.where(mine, dop, zero))
        s = dot(jnp.concatenate([km[h], jnp.broadcast_to(sel, kp.shape).astype(bf16)], 1), qa, 1, 1)
        dp = dot(jnp.concatenate([vm, jnp.broadcast_to(sel_d, kp.shape).astype(bf16)], 1), da, 1, 1)
        p = jnp.exp2(s * EXP_SCALE)
        if rank_row is not None:
            p = jnp.where(rank_row >= rank_col, p, 0.0)
        pb.append(p.astype(bf16))
        db.append((p * dp).astype(bf16))
    dv = dot(jnp.concatenate(pb, 1), jnp.concatenate(dm, 0), 1, 0)
    dk = dot(jnp.concatenate(db, 1), jnp.concatenate(qm, 0), 1, 0)
    dq = dot(jnp.concatenate(db, 0), jnp.concatenate(km, 0), 0, 0)
    return dq, dk, dv


def pairs(body):
    def step(hp, _):
        body(hp, pl.ds(pl.multiple_of(hp * PAIR, PAIR), PAIR), pl.ds(pl.multiple_of(WC + hp * PAIR, PAIR), PAIR))
        return 0

    lax.fori_loop(0, HC // 2, step, 0)


def diag_kernel(c, q, qa, kv, rank, dq, dkv):
    rank_col = jnp.broadcast_to(rank[:1], (128, rank.shape[1])).T[:, :1]

    def body(hp, at, at2):
        x, y, z = tile(q, qa[:, 2 * WC :], kv, c, hp, None, rank[:1], rank_col)
        dq[:, at] = x
        dkv[:, at] = y
        dkv[:, at2] = z

    pairs(body)


def cross_kernel(c, odd, q0, a0, q1, a1, k0, k1, dq, dkv, *refs):
    before, (dq_out, dkv_out, dq1, dkv1) = refs[:-4], refs[-4:]
    near = jnp.where(odd[0] & 1 == 0, 3, 1)

    base = 0
    for part in before:
        dq1[:, base : base + WC] = part[...]
        base += WC

    def body(hp, at, at2):
        x, y, z = tile(q0, a0[:, 2 * WC :], k1, c, hp, 2)
        dq_out[:, at] = dq[:, at] + x
        x, y2, z2 = tile(q1, a1[:, 2 * WC :], k1, c, hp, near)
        dkv1[:, at] = y + y2
        dkv1[:, at2] = z + z2
        to = pl.ds(pl.multiple_of(base + hp * PAIR, PAIR), PAIR)

        @pl.when(odd[0] & 1 == 0)
        def _():
            x3, y3, z3 = tile(q1, a1[:, 2 * WC :], k0, c, hp, 1)
            dq1[:, to] = ((x + x3) * 0.125).astype(bf16)
            dkv_out[:, at] = dkv[:, at] + y3
            dkv_out[:, at2] = dkv[:, at2] + z3

        @pl.when(odd[0] & 1 != 0)
        def _():
            dq1[:, to] = (x * 0.125).astype(bf16)
            dkv_out[:, at] = dkv[:, at]
            dkv_out[:, at2] = dkv[:, at2]

    pairs(body)


def last_kernel(c, odd, q2_far, a2_far, k1, edge, dkv1, *refs):
    before, (dq2, out, q2) = refs[:-3], refs[-3:]
    a2 = q2 if c == 0 else a2_far

    @pl.when(odd[0] & 8 != 0)
    def _():
        q2[...] = edge[...]


    base = 0
    for part in before:
        dq2[:, base : base + WC] = part[...]
        base += WC

    def body(hp, at, at2):
        to = pl.ds(pl.multiple_of(base + hp * PAIR, PAIR), PAIR)

        @pl.when(odd[0] & 1 != 0)
        def _():
            x, y, z = tile(q2, a2[:, 2 * WC :], k1, c, hp, 3)
            dq2[:, to] = (x * 0.125).astype(bf16)
            out[:, at] = ((dkv1[:, at] + y) * 0.125).astype(bf16)
            out[:, at2] = (dkv1[:, at2] + z).astype(bf16)

        @pl.when(odd[0] & 1 == 0)
        def _():
            dq2[:, to] = jnp.zeros((dq2.shape[0], PAIR), bf16)
            out[:, at] = (dkv1[:, at] * 0.125).astype(bf16)
            out[:, at2] = dkv1[:, at2].astype(bf16)

    pairs(body)


def first_sum(dq_a, dq_b, dkv, r1, r2, back, gq, gk, gv):
    far = r1[...].astype(f32) + r2[...].astype(f32)
    gq[:, :WC] = (dq_a[...] * 0.125 + far[:, :WC]).astype(bf16)
    gq[:, WC:] = (dq_b[...] * 0.125 + far[:, WC:]).astype(bf16)
    gk[...] = (dkv[:, :WC] * 0.125 + back[:, :WC].astype(f32)).astype(bf16)
    gv[...] = (dkv[:, WC:] + back[:, WC:].astype(f32)).astype(bf16)


def last_sum(pk, pv, dkv, back, gk, gv):
    gk[:, :WC] = pk[...]
    gv[:, :WC] = pv[...]
    gk[:, WC:] = (dkv[:, :WC] * 0.125 + back[:, :WC].astype(f32)).astype(bf16)
    gv[:, WC:] = (dkv[:, WC:] + back[:, WC:].astype(f32)).astype(bf16)


VM = pl.BlockSpec(memory_space=pltpu.VMEM)
SM = pl.BlockSpec(memory_space=pltpu.SMEM)


def call(kernel, outs, n_smem, args, scratch=(), flops=0, n_far=0, vmem=16, alias=None):
    near = len(args) - n_smem - n_far
    return pl.pallas_call(
        kernel,
        out_shape=outs,
        in_specs=[SM] * n_smem + [VM] * near + [pl.BlockSpec(memory_space=pltpu.HBM)] * n_far,
        out_specs=[VM] * len(outs),
        scratch_shapes=list(scratch),
        input_output_aliases=alias or {},
        cost_estimate=pl.CostEstimate(flops=flops, bytes_accessed=1 << 10, transcendentals=0),
        compiler_params=pltpu.CompilerParams(vmem_limit_bytes=vmem << 20),
    )(*args)


def per_device(query, keys, values, output, grad_output, log_sum_exp, order, layout):
    rows = query.shape[0]
    n = lax.axis_size(AXES)
    block = lax.axis_index(AXES)
    blk = jnp.reshape(block, (1,)).astype(jnp.int32)
    parity, place = block % 2, block % SPAN
    takes = jnp.where((place == SPAN - 1) & (block < n - 1), 8, 0)
    odd = jnp.reshape(parity + takes, (1,)).astype(jnp.int32)
    edges = range(SPAN, n, SPAN)

    def arr(cols, kind):
        return jax.ShapeDtypeStruct((rows, cols), kind)

    def shifted(x, by, keep=lambda i: True):
        return lax.ppermute(x, AXES, [(i - by, i) for i in range(n) if 0 <= i - by < n and keep(i)])

    def swapped(x):
        return lax.ppermute(x, AXES, [(i ^ 1, i) for i in range(n)])

    tile_flops = COST * 5 * 2 * rows * rows * SIZE * HEADS
    qw = [2 * WC + (128 if c == 0 else 0) for c in range(CHUNKS)]
    kv = jnp.concatenate([keys, values], 1)
    k1 = shifted(kv, 2)
    kv, query = lax.optimization_barrier((kv, query))
    *q0, rank = call(
        pack_q,
        [arr(w, bf16) for w in qw] + [jax.ShapeDtypeStruct((8, rows), f32)],
        2,
        (blk, layout, log_sum_exp, order, jnp.concatenate([query, grad_output, output], 1)),
    )
    q1 = [swapped(q0[c]) for c in range(CHUNKS)]
    edge = [lax.ppermute(q0[c], AXES, [(s, s - 1) for s in edges]) for c in range(CHUNKS)]
    a0 = q0[0]
    dqs, dkvs, back_kv, dq1, dq2, parts = [], [], [], (), (), []
    diag = []
    for c in range(CHUNKS):
        diag.append(
            call(
                functools.partial(diag_kernel, c),
                [arr(WC, f32), arr(2 * WC, f32)],
                0,
                (q0[c], a0, kv, rank),
                flops=tile_flops // CHUNKS,
            )
        )
    q1[0], diag = lax.optimization_barrier((q1[0], diag))
    q2 = [shifted(q1[0], -2, lambda i: i % 2 == 1 and i % SPAN != SPAN - 1)]
    a1 = q1[0]
    for c in range(CHUNKS):
        dq, dkv = diag[c]
        dq, dkv, x, dkv1 = call(
            functools.partial(cross_kernel, c),
            [arr(WC, f32), arr(2 * WC, f32), arr((c + 1) * WC, bf16), arr(2 * WC, f32)],
            1,
            (odd, q0[c], a0, q1[c], a1, kv, k1, dq, dkv, *dq1),
            flops=3 * tile_flops // CHUNKS,
        )
        dq1 = (x,)
        dqs.append(dq)
        dkvs.append(dkv)
        parts.append(dkv1)
        if c == 0:
            q1[1], dq1 = lax.optimization_barrier((q1[1], dq1))
            q2.append(shifted(q1[1], -2, lambda i: i % 2 == 1 and i % SPAN != SPAN - 1))
    back_q1 = swapped(dq1[0])
    q2[0], tail = lax.optimization_barrier((q2[0], dq1[0]))
    for c in range(CHUNKS):
        dkv1 = parts[c]
        x, send, q2[c] = call(
            functools.partial(last_kernel, c),
            [arr((c + 1) * WC, bf16), arr(2 * WC, bf16), arr(qw[c], bf16)],
            1,
            (odd, q2[c], q2[0], k1, edge[c], dkv1, *dq2),
            flops=0,
            alias={1: 2},
        )
        dq2 = (x,)
        back_kv.append(shifted(send, -2))
    back_q2 = lax.ppermute(dq2[0], AXES, [(i, i + 1) for i in range(1, n - 1, 2)])
    gq, pk, pv = call(
        first_sum,
        [arr(HEADS * SIZE, bf16), arr(WC, bf16), arr(WC, bf16)],
        0,
        (*dqs, dkvs[0], back_q1, back_q2, back_kv[0]),
        flops=20 << 30,
    )
    gk, gv = call(last_sum, [arr(HEADS * SIZE, bf16)] * 2, 0, (pk, pv, dkvs[1], back_kv[1]), flops=1 << 20)
    return gq, gk, gv


def solution(mesh):
    rows = P(AXES, None)
    return jax.shard_map(
        per_device,
        mesh=mesh,
        in_specs=(rows, rows, rows, rows, rows, P(None, AXES), rows, rows),
        out_specs=(rows, rows, rows),
        check_vma=False,
    )
```

```python
import functools
import math

import jax
import jax.numpy as jnp
from jax import lax
from jax.experimental import pallas as pl
from jax.experimental.pallas import tpu as pltpu
from jax.sharding import PartitionSpec as P

AXES = ("inner", "outer")
HEADS = 8
SIZE = 64
PAIR = 2 * SIZE
CHUNKS = 2
COST = 8
SPAN = 128
HC = HEADS // CHUNKS
WC = HC * SIZE
EXP_SCALE = 0.125 / math.log(2.0)
HIDDEN = -1e30
f32 = jnp.float32
bf16 = jnp.bfloat16

VIS = 48


def dot(a, b, ca, cb):
    return lax.dot_general(a, b, (((ca,), (cb,)), ((), ())), preferred_element_type=f32)


def pieces(x):
    a = x.astype(bf16)
    r = x - a.astype(f32)
    b = r.astype(bf16)
    c = (r - b.astype(f32)).astype(bf16)
    return a, b, c


def pack_q(blk, layout, lse, order, everything, *outs):
    q, do, o = (everything.at[:, i * HEADS * SIZE : (i + 1) * HEADS * SIZE] for i in range(3))
    qs, rank = outs[:CHUNKS], outs[CHUNKS]
    rows = q.shape[0]
    for c in range(CHUNKS):
        w = slice(c * WC, (c + 1) * WC)
        qs[c][:, :WC] = q[:, w]
        qs[c][:, WC : 2 * WC] = do[:, w]
    lane = lax.broadcasted_iota(jnp.int32, (1, 128), 1)
    prod = do[...].astype(f32) * o[...].astype(f32)
    hi = prod.astype(bf16)
    lo = (prod - hi.astype(f32)).astype(bf16)
    feat = lax.broadcasted_iota(jnp.int32, (HEADS * SIZE, 128), 0) // SIZE
    flane = lax.broadcasted_iota(jnp.int32, (HEADS * SIZE, 128), 1)
    pick = jnp.where((flane % 8 == feat) & (flane >= 24) & (flane < 48), 1.0, 0.0).astype(bf16)
    delta = dot(hi, pick, 1, 0) + dot(lo, pick, 1, 0)
    d1, d2, d3 = (x.astype(f32) for x in pieces(delta))
    dpart = jnp.where(lane < 32, d1, jnp.where(lane < 40, d2, d3))
    l1, l2, l3 = (x.astype(f32) for x in pieces(lse[...] * 8.0))
    stack = jnp.concatenate([l1, l2, l3, jnp.zeros_like(l1)], 0).astype(bf16)
    r = lax.broadcasted_iota(jnp.int32, (32, 128), 0)
    c = lax.broadcasted_iota(jnp.int32, (32, 128), 1)
    eye = jnp.where((r == c) & (r < 24), 1.0, 0.0).astype(bf16)
    lpart = dot(stack, eye, 0, 0)
    vis = jnp.zeros((1, 128), f32)
    for d in (1, 2, 3):
        seen = jnp.logical_and(layout[0, d - 1] > 0, blk[0] >= d)
        vis = jnp.where((lane == VIS + d - 1) & jnp.logical_not(seen), f32(HIDDEN), vis)
    aux = jnp.where(lane < 24, lpart, jnp.where(lane < 48, dpart, jnp.broadcast_to(vis, (rows, 128))))
    qs[0][:, 2 * WC :] = aux.astype(bf16)
    rank[...] = jnp.broadcast_to(order[...].astype(f32), rank.shape)


def tile(q, aux, kv, c, hp, dist, rank_row=None, rank_col=None):
    at = pl.ds(pl.multiple_of(hp * PAIR, PAIR), PAIR)
    at2 = pl.ds(pl.multiple_of(WC + hp * PAIR, PAIR), PAIR)
    at_k = pl.ds(pl.multiple_of(c * WC + hp * PAIR, PAIR), PAIR)
    at_v = pl.ds(pl.multiple_of((CHUNKS + c) * WC + hp * PAIR, PAIR), PAIR)
    qp, dop, kp, vp = q[:, at], q[:, at2], kv[:, at_k], kv[:, at_v]
    lane = lax.broadcasted_iota(jnp.int32, (1, PAIR), 1)
    half = lax.broadcasted_iota(jnp.int32, qp.shape, 1) // SIZE
    qa = jnp.concatenate([qp, aux], 1)
    da = jnp.concatenate([dop, aux], 1)
    km, qm, dm, vm, sels, seld = [], [], [], [], [], []
    rows = qp.shape[0]
    for h in range(2):
        head = c * HC + hp * 2 + h
        sel = jnp.where((lane % 8 == head) & (lane < 24), -1.0, 0.0)
        if dist is not None:
            sel = jnp.where(lane == VIS - 1 + dist, 1.0, sel)
        sel_d = jnp.where((lane % 8 == head) & (lane >= 24) & (lane < 48), -1.0, 0.0)
        mine = half == h
        zero = jnp.zeros_like(kp)
        km.append(jnp.where(mine, kp, zero))
        vm.append(jnp.where(mine, vp, zero))
        qm.append(jnp.where(mine, qp, zero))
        dm.append(jnp.where(mine, dop, zero))
        sels.append(jnp.broadcast_to(sel, kp.shape).astype(bf16))
        seld.append(jnp.broadcast_to(sel_d, kp.shape).astype(bf16))
    k_both = jnp.concatenate(km, 0)
    s = dot(jnp.concatenate([k_both, jnp.concatenate(sels, 0)], 1), qa, 1, 1)
    dp = dot(jnp.concatenate([jnp.concatenate(vm, 0), jnp.concatenate(seld, 0)], 1), da, 1, 1)
    p = jnp.exp2(s * EXP_SCALE)
    if rank_row is not None:
        seen = rank_row >= rank_col
        p = jnp.where(jnp.concatenate([seen, seen], 0), p, 0.0)
    p_low, ds = p.astype(bf16), (p * dp).astype(bf16)
    pb, db = [p_low[:rows], p_low[rows:]], [ds[:rows], ds[rows:]]
    dv = dot(jnp.concatenate(pb, 1), jnp.concatenate(dm, 0), 1, 0)
    dk = dot(jnp.concatenate(db, 1), jnp.concatenate(qm, 0), 1, 0)
    dq = dot(k_both, ds, 0, 0).T
    return dq, dk, dv


def pairs(body):
    def step(hp, _):
        body(hp, pl.ds(pl.multiple_of(hp * PAIR, PAIR), PAIR), pl.ds(pl.multiple_of(WC + hp * PAIR, PAIR), PAIR))
        return 0

    lax.fori_loop(0, HC // 2, step, 0)


def diag_kernel(c, q, qa, kv, rank, dq, dkv):
    rank_col = jnp.broadcast_to(rank[:1], (128, rank.shape[1])).T[:, :1]

    def body(hp, at, at2):
        x, y, z = tile(q, qa[:, 2 * WC :], kv, c, hp, None, rank[:1], rank_col)
        dq[:, at] = x
        dkv[:, at] = y
        dkv[:, at2] = z

    pairs(body)


def cross_kernel(c, odd, q0, a0, q1, a1, k0, k1, dq, dkv, *refs):
    before, (dq_out, dkv_out, dq1, dkv1) = refs[:-4], refs[-4:]
    near = jnp.where(odd[0] & 1 == 0, 3, 1)

    base = 0
    for part in before:
        dq1[:, base : base + WC] = part[...]
        base += WC

    def body(hp, at, at2):
        x, y, z = tile(q0, a0[:, 2 * WC :], k1, c, hp, 2)
        dq_out[:, at] = dq[:, at] + x
        x, y2, z2 = tile(q1, a1[:, 2 * WC :], k1, c, hp, near)
        dkv1[:, at] = y + y2
        dkv1[:, at2] = z + z2
        to = pl.ds(pl.multiple_of(base + hp * PAIR, PAIR), PAIR)

        @pl.when(odd[0] & 1 == 0)
        def _():
            x3, y3, z3 = tile(q1, a1[:, 2 * WC :], k0, c, hp, 1)
            dq1[:, to] = ((x + x3) * 0.125).astype(bf16)
            dkv_out[:, at] = dkv[:, at] + y3
            dkv_out[:, at2] = dkv[:, at2] + z3

        @pl.when(odd[0] & 1 != 0)
        def _():
            dq1[:, to] = (x * 0.125).astype(bf16)
            dkv_out[:, at] = dkv[:, at]
            dkv_out[:, at2] = dkv[:, at2]

    pairs(body)


def last_kernel(c, odd, q2_far, a2_far, k1, edge, dkv1, *refs):
    before, (dq2, out, q2) = refs[:-3], refs[-3:]
    a2 = q2 if c == 0 else a2_far

    @pl.when(odd[0] & 8 != 0)
    def _():
        q2[...] = edge[...]


    base = 0
    for part in before:
        dq2[:, base : base + WC] = part[...]
        base += WC

    def body(hp, at, at2):
        to = pl.ds(pl.multiple_of(base + hp * PAIR, PAIR), PAIR)

        @pl.when(odd[0] & 1 != 0)
        def _():
            x, y, z = tile(q2, a2[:, 2 * WC :], k1, c, hp, 3)
            dq2[:, to] = (x * 0.125).astype(bf16)
            out[:, at] = ((dkv1[:, at] + y) * 0.125).astype(bf16)
            out[:, at2] = (dkv1[:, at2] + z).astype(bf16)

        @pl.when(odd[0] & 1 == 0)
        def _():
            dq2[:, to] = jnp.zeros((dq2.shape[0], PAIR), bf16)
            out[:, at] = (dkv1[:, at] * 0.125).astype(bf16)
            out[:, at2] = dkv1[:, at2].astype(bf16)

    pairs(body)


def first_sum(dq_a, dq_b, dkv, r1, r2, back, gq, gk, gv):
    far = r1[...].astype(f32) + r2[...].astype(f32)
    gq[:, :WC] = (dq_a[...] * 0.125 + far[:, :WC]).astype(bf16)
    gq[:, WC:] = (dq_b[...] * 0.125 + far[:, WC:]).astype(bf16)
    gk[...] = (dkv[:, :WC] * 0.125 + back[:, :WC].astype(f32)).astype(bf16)
    gv[...] = (dkv[:, WC:] + back[:, WC:].astype(f32)).astype(bf16)


def last_sum(pk, pv, dkv, back, gk, gv):
    gk[:, :WC] = pk[...]
    gv[:, :WC] = pv[...]
    gk[:, WC:] = (dkv[:, :WC] * 0.125 + back[:, :WC].astype(f32)).astype(bf16)
    gv[:, WC:] = (dkv[:, WC:] + back[:, WC:].astype(f32)).astype(bf16)


VM = pl.BlockSpec(memory_space=pltpu.VMEM)
SM = pl.BlockSpec(memory_space=pltpu.SMEM)


def call(kernel, outs, n_smem, args, scratch=(), flops=0, n_far=0, vmem=16, alias=None):
    near = len(args) - n_smem - n_far
    return pl.pallas_call(
        kernel,
        out_shape=outs,
        in_specs=[SM] * n_smem + [VM] * near + [pl.BlockSpec(memory_space=pltpu.HBM)] * n_far,
        out_specs=[VM] * len(outs),
        scratch_shapes=list(scratch),
        input_output_aliases=alias or {},
        cost_estimate=pl.CostEstimate(flops=flops, bytes_accessed=1 << 10, transcendentals=0),
        compiler_params=pltpu.CompilerParams(vmem_limit_bytes=vmem << 20),
    )(*args)


def per_device(query, keys, values, output, grad_output, log_sum_exp, order, layout):
    rows = query.shape[0]
    n = lax.axis_size(AXES)
    block = lax.axis_index(AXES)
    blk = jnp.reshape(block, (1,)).astype(jnp.int32)
    parity, place = block % 2, block % SPAN
    takes = jnp.where((place == SPAN - 1) & (block < n - 1), 8, 0)
    odd = jnp.reshape(parity + takes, (1,)).astype(jnp.int32)
    edges = range(SPAN, n, SPAN)

    def arr(cols, kind):
        return jax.ShapeDtypeStruct((rows, cols), kind)

    def shifted(x, by, keep=lambda i: True):
        return lax.ppermute(x, AXES, [(i - by, i) for i in range(n) if 0 <= i - by < n and keep(i)])

    def swapped(x):
        return lax.ppermute(x, AXES, [(i ^ 1, i) for i in range(n)])

    tile_flops = COST * 5 * 2 * rows * rows * SIZE * HEADS
    qw = [2 * WC + (128 if c == 0 else 0) for c in range(CHUNKS)]
    kv = jnp.concatenate([keys, values], 1)
    k1 = shifted(kv, 2)
    kv, query = lax.optimization_barrier((kv, query))
    *q0, rank = call(
        pack_q,
        [arr(w, bf16) for w in qw] + [jax.ShapeDtypeStruct((8, rows), f32)],
        2,
        (blk, layout, log_sum_exp, order, jnp.concatenate([query, grad_output, output], 1)),
    )
    q1 = [swapped(q0[c]) for c in range(CHUNKS)]
    edge = [lax.ppermute(q0[c], AXES, [(s, s - 1) for s in edges]) for c in range(CHUNKS)]
    a0 = q0[0]
    dqs, dkvs, back_kv, dq1, dq2, parts = [], [], [], (), (), []
    diag = []
    for c in range(CHUNKS):
        diag.append(
            call(
                functools.partial(diag_kernel, c),
                [arr(WC, f32), arr(2 * WC, f32)],
                0,
                (q0[c], a0, kv, rank),
                flops=tile_flops // CHUNKS,
            )
        )
    q1[0], diag = lax.optimization_barrier((q1[0], diag))
    q2 = [shifted(q1[0], -2, lambda i: i % 2 == 1 and i % SPAN != SPAN - 1)]
    a1 = q1[0]
    for c in range(CHUNKS):
        dq, dkv = diag[c]
        dq, dkv, x, dkv1 = call(
            functools.partial(cross_kernel, c),
            [arr(WC, f32), arr(2 * WC, f32), arr((c + 1) * WC, bf16), arr(2 * WC, f32)],
            1,
            (odd, q0[c], a0, q1[c], a1, kv, k1, dq, dkv, *dq1),
            flops=3 * tile_flops // CHUNKS,
        )
        dq1 = (x,)
        dqs.append(dq)
        dkvs.append(dkv)
        parts.append(dkv1)
        if c == 0:
            q1[1], dq1 = lax.optimization_barrier((q1[1], dq1))
            q2.append(shifted(q1[1], -2, lambda i: i % 2 == 1 and i % SPAN != SPAN - 1))
    for c in range(CHUNKS):
        dkv1 = parts[c]
        x, send, q2[c] = call(
            functools.partial(last_kernel, c),
            [arr((c + 1) * WC, bf16), arr(2 * WC, bf16), arr(qw[c], bf16)],
            1,
            (odd, q2[c], q2[0], k1, edge[c], dkv1, *dq2),
            flops=0,
            alias={1: 2},
        )
        dq2 = (x,)
        if c == 0:
            dq1, dq2, q2[1] = lax.optimization_barrier((dq1, dq2, q2[1]))
            back_q1 = swapped(dq1[0])
        back_kv.append(shifted(send, -2))
    back_q2 = lax.ppermute(dq2[0], AXES, [(i, i + 1) for i in range(1, n - 1, 2)])
    gq, pk, pv = call(
        first_sum,
        [arr(HEADS * SIZE, bf16), arr(WC, bf16), arr(WC, bf16)],
        0,
        (*dqs, dkvs[0], back_q1, back_q2, back_kv[0]),
        flops=20 << 30,
    )
    gk, gv = call(last_sum, [arr(HEADS * SIZE, bf16)] * 2, 0, (pk, pv, dkvs[1], back_kv[1]), flops=1 << 20)
    return gq, gk, gv


def solution(mesh):
    rows = P(AXES, None)
    return jax.shard_map(
        per_device,
        mesh=mesh,
        in_specs=(rows, rows, rows, rows, rows, P(None, AXES), rows, rows),
        out_specs=(rows, rows, rows),
        check_vma=False,
    )
```

```python
import functools
import math

import jax
import jax.numpy as jnp
from jax import lax
from jax.experimental import pallas as pl
from jax.experimental.pallas import tpu as pltpu
from jax.sharding import PartitionSpec as P

AXES = ("inner", "outer")
HEADS = 8
SIZE = 64
PAIR = 2 * SIZE
CHUNKS = 2
COST = 8
SPAN = 128
HC = HEADS // CHUNKS
WC = HC * SIZE
EXP_SCALE = 0.125 / math.log(2.0)
HIDDEN = -1e30
f32 = jnp.float32
bf16 = jnp.bfloat16

VIS = 48


def dot(a, b, ca, cb):
    return lax.dot_general(a, b, (((ca,), (cb,)), ((), ())), preferred_element_type=f32)


def pieces(x):
    a = x.astype(bf16)
    r = x - a.astype(f32)
    b = r.astype(bf16)
    c = (r - b.astype(f32)).astype(bf16)
    return a, b, c


def pack_q(blk, layout, lse, order, everything, *outs):
    q, do, o = (everything.at[:, i * HEADS * SIZE : (i + 1) * HEADS * SIZE] for i in range(3))
    qs, rank = outs[:CHUNKS], outs[CHUNKS]
    rows = q.shape[0]
    for c in range(CHUNKS):
        w = slice(c * WC, (c + 1) * WC)
        qs[c][:, :WC] = q[:, w]
        qs[c][:, WC : 2 * WC] = do[:, w]
    lane = lax.broadcasted_iota(jnp.int32, (1, 128), 1)
    prod = do[...].astype(f32) * o[...].astype(f32)
    hi = prod.astype(bf16)
    lo = (prod - hi.astype(f32)).astype(bf16)
    feat = lax.broadcasted_iota(jnp.int32, (HEADS * SIZE, 128), 0) // SIZE
    flane = lax.broadcasted_iota(jnp.int32, (HEADS * SIZE, 128), 1)
    pick = jnp.where((flane % 8 == feat) & (flane >= 24) & (flane < 48), 1.0, 0.0).astype(bf16)
    delta = dot(hi, pick, 1, 0) + dot(lo, pick, 1, 0)
    d1, d2, d3 = (x.astype(f32) for x in pieces(delta))
    dpart = jnp.where(lane < 32, d1, jnp.where(lane < 40, d2, d3))
    l1, l2, l3 = (x.astype(f32) for x in pieces(lse[...] * 8.0))
    stack = jnp.concatenate([l1, l2, l3, jnp.zeros_like(l1)], 0).astype(bf16)
    r = lax.broadcasted_iota(jnp.int32, (32, 128), 0)
    c = lax.broadcasted_iota(jnp.int32, (32, 128), 1)
    eye = jnp.where((r == c) & (r < 24), 1.0, 0.0).astype(bf16)
    lpart = dot(stack, eye, 0, 0)
    vis = jnp.zeros((1, 128), f32)
    for d in (1, 2, 3):
        seen = jnp.logical_and(layout[0, d - 1] > 0, blk[0] >= d)
        vis = jnp.where((lane == VIS + d - 1) & jnp.logical_not(seen), f32(HIDDEN), vis)
    aux = jnp.where(lane < 24, lpart, jnp.where(lane < 48, dpart, jnp.broadcast_to(vis, (rows, 128))))
    qs[0][:, 2 * WC :] = aux.astype(bf16)
    rank[...] = jnp.broadcast_to(order[...].astype(f32), rank.shape)


def tile(q, aux, kv, c, hp, dist, rank_row=None, rank_col=None):
    at = pl.ds(pl.multiple_of(hp * PAIR, PAIR), PAIR)
    at2 = pl.ds(pl.multiple_of(WC + hp * PAIR, PAIR), PAIR)
    at_k = pl.ds(pl.multiple_of(c * WC + hp * PAIR, PAIR), PAIR)
    at_v = pl.ds(pl.multiple_of((CHUNKS + c) * WC + hp * PAIR, PAIR), PAIR)
    qp, dop, kp, vp = q[:, at], q[:, at2], kv[:, at_k], kv[:, at_v]
    lane = lax.broadcasted_iota(jnp.int32, (1, PAIR), 1)
    half = lax.broadcasted_iota(jnp.int32, qp.shape, 1) // SIZE
    qa = jnp.concatenate([qp, aux], 1)
    da = jnp.concatenate([dop, aux], 1)
    km, qm, dm, vm, sels, seld = [], [], [], [], [], []
    rows = qp.shape[0]
    for h in range(2):
        head = c * HC + hp * 2 + h
        sel = jnp.where((lane % 8 == head) & (lane < 24), -1.0, 0.0)
        if dist is not None:
            sel = jnp.where(lane == VIS - 1 + dist, 1.0, sel)
        sel_d = jnp.where((lane % 8 == head) & (lane >= 24) & (lane < 48), -1.0, 0.0)
        mine = half == h
        zero = jnp.zeros_like(kp)
        km.append(jnp.where(mine, kp, zero))
        vm.append(jnp.where(mine, vp, zero))
        qm.append(jnp.where(mine, qp, zero))
        dm.append(jnp.where(mine, dop, zero))
        sels.append(jnp.broadcast_to(sel, kp.shape).astype(bf16))
        seld.append(jnp.broadcast_to(sel_d, kp.shape).astype(bf16))
    k_both = jnp.concatenate(km, 0)
    s = dot(jnp.concatenate([k_both, jnp.concatenate(sels, 0)], 1), qa, 1, 1)
    dp = dot(jnp.concatenate([jnp.concatenate(vm, 0), jnp.concatenate(seld, 0)], 1), da, 1, 1)
    p = jnp.exp2(s * EXP_SCALE)
    if rank_row is not None:
        seen = rank_row >= rank_col
        p = jnp.where(jnp.concatenate([seen, seen], 0), p, 0.0)
    p_low, ds = p.astype(bf16), (p * dp).astype(bf16)
    pb, db = [p_low[:rows], p_low[rows:]], [ds[:rows], ds[rows:]]
    dv = dot(jnp.concatenate(pb, 1), jnp.concatenate(dm, 0), 1, 0)
    dk = dot(jnp.concatenate(db, 1), jnp.concatenate(qm, 0), 1, 0)
    dq = dot(k_both, ds, 0, 0).T
    return dq, dk, dv


def pairs(body):
    def step(hp, _):
        body(hp, pl.ds(pl.multiple_of(hp * PAIR, PAIR), PAIR), pl.ds(pl.multiple_of(WC + hp * PAIR, PAIR), PAIR))
        return 0

    lax.fori_loop(0, HC // 2, step, 0)


def diag_kernel(c, q, qa, kv, rank, dq, dkv):
    rank_col = jnp.broadcast_to(rank[:1], (128, rank.shape[1])).T[:, :1]

    def body(hp, at, at2):
        x, y, z = tile(q, qa[:, 2 * WC :], kv, c, hp, None, rank[:1], rank_col)
        dq[:, at] = x
        dkv[:, at] = y
        dkv[:, at2] = z

    pairs(body)


def cross_kernel(c, odd, q0, a0, q1, a1, k0, k1, dq, dkv, *refs):
    before, (dq_out, dkv_out, dq1, dkv1) = refs[:-4], refs[-4:]
    near = jnp.where(odd[0] & 1 == 0, 3, 1)

    base = 0
    for part in before:
        dq1[:, base : base + WC] = part[...]
        base += WC

    def body(hp, at, at2):
        x, y, z = tile(q0, a0[:, 2 * WC :], k1, c, hp, 2)
        dq_out[:, at] = dq[:, at] + x
        x, y2, z2 = tile(q1, a1[:, 2 * WC :], k1, c, hp, near)
        dkv1[:, at] = y + y2
        dkv1[:, at2] = z + z2
        to = pl.ds(pl.multiple_of(base + hp * PAIR, PAIR), PAIR)

        @pl.when(odd[0] & 1 == 0)
        def _():
            x3, y3, z3 = tile(q1, a1[:, 2 * WC :], k0, c, hp, 1)
            dq1[:, to] = ((x + x3) * 0.125).astype(bf16)
            dkv_out[:, at] = dkv[:, at] + y3
            dkv_out[:, at2] = dkv[:, at2] + z3

        @pl.when(odd[0] & 1 != 0)
        def _():
            dq1[:, to] = (x * 0.125).astype(bf16)
            dkv_out[:, at] = dkv[:, at]
            dkv_out[:, at2] = dkv[:, at2]

    pairs(body)


def last_kernel(c, odd, q2_far, a2_far, k1, edge, dkv1, *refs):
    before, (dq2, out, q2) = refs[:-3], refs[-3:]
    a2 = q2 if c == 0 else a2_far

    @pl.when(odd[0] & 8 != 0)
    def _():
        q2[...] = edge[...]


    base = 0
    if before:
        base = WC
        dq2[:, :WC] = before[0][...]
        out[:, : 2 * WC] = before[1][...]

    def body(hp, at, at2):
        to = pl.ds(pl.multiple_of(base + hp * PAIR, PAIR), PAIR)
        to_k = pl.ds(pl.multiple_of(2 * base + hp * PAIR, PAIR), PAIR)
        to_v = pl.ds(pl.multiple_of(2 * base + WC + hp * PAIR, PAIR), PAIR)

        @pl.when(odd[0] & 1 != 0)
        def _():
            x, y, z = tile(q2, a2[:, 2 * WC :], k1, c, hp, 3)
            dq2[:, to] = (x * 0.125).astype(bf16)
            out[:, to_k] = ((dkv1[:, at] + y) * 0.125).astype(bf16)
            out[:, to_v] = (dkv1[:, at2] + z).astype(bf16)

        @pl.when(odd[0] & 1 == 0)
        def _():
            dq2[:, to] = jnp.zeros((dq2.shape[0], PAIR), bf16)
            out[:, to_k] = (dkv1[:, at] * 0.125).astype(bf16)
            out[:, to_v] = dkv1[:, at2].astype(bf16)

    pairs(body)


def sum_q(dq_a, dq_b, r1, r2, gq):
    far = r1[...].astype(f32) + r2[...].astype(f32)
    gq[:, :WC] = (dq_a[...] * 0.125 + far[:, :WC]).astype(bf16)
    gq[:, WC:] = (dq_b[...] * 0.125 + far[:, WC:]).astype(bf16)


def sum_kv(dkv_a, dkv_b, back, gk, gv):
    for c, dkv in enumerate((dkv_a, dkv_b)):
        w = slice(c * WC, (c + 1) * WC)
        k_at = slice(2 * c * WC, (2 * c + 1) * WC)
        v_at = slice((2 * c + 1) * WC, (2 * c + 2) * WC)
        gk[:, w] = (dkv[:, :WC] * 0.125 + back[:, k_at].astype(f32)).astype(bf16)
        gv[:, w] = (dkv[:, WC:] + back[:, v_at].astype(f32)).astype(bf16)


VM = pl.BlockSpec(memory_space=pltpu.VMEM)
SM = pl.BlockSpec(memory_space=pltpu.SMEM)


def call(kernel, outs, n_smem, args, scratch=(), flops=0, n_far=0, vmem=16, alias=None):
    near = len(args) - n_smem - n_far
    return pl.pallas_call(
        kernel,
        out_shape=outs,
        in_specs=[SM] * n_smem + [VM] * near + [pl.BlockSpec(memory_space=pltpu.HBM)] * n_far,
        out_specs=[VM] * len(outs),
        scratch_shapes=list(scratch),
        input_output_aliases=alias or {},
        cost_estimate=pl.CostEstimate(flops=flops, bytes_accessed=1 << 10, transcendentals=0),
        compiler_params=pltpu.CompilerParams(vmem_limit_bytes=vmem << 20),
    )(*args)


def per_device(query, keys, values, output, grad_output, log_sum_exp, order, layout):
    rows = query.shape[0]
    n = lax.axis_size(AXES)
    block = lax.axis_index(AXES)
    blk = jnp.reshape(block, (1,)).astype(jnp.int32)
    parity, place = block % 2, block % SPAN
    takes = jnp.where((place == SPAN - 1) & (block < n - 1), 8, 0)
    odd = jnp.reshape(parity + takes, (1,)).astype(jnp.int32)
    edges = range(SPAN, n, SPAN)

    def arr(cols, kind):
        return jax.ShapeDtypeStruct((rows, cols), kind)

    def shifted(x, by, keep=lambda i: True):
        return lax.ppermute(x, AXES, [(i - by, i) for i in range(n) if 0 <= i - by < n and keep(i)])

    def swapped(x):
        return lax.ppermute(x, AXES, [(i ^ 1, i) for i in range(n)])

    tile_flops = COST * 5 * 2 * rows * rows * SIZE * HEADS
    qw = [2 * WC + (128 if c == 0 else 0) for c in range(CHUNKS)]
    kv = jnp.concatenate([keys, values], 1)
    k1 = shifted(kv, 2)
    kv, query = lax.optimization_barrier((kv, query))
    *q0, rank = call(
        pack_q,
        [arr(w, bf16) for w in qw] + [jax.ShapeDtypeStruct((8, rows), f32)],
        2,
        (blk, layout, log_sum_exp, order, jnp.concatenate([query, grad_output, output], 1)),
    )
    q1 = [swapped(q0[c]) for c in range(CHUNKS)]
    edge = [lax.ppermute(q0[c], AXES, [(s, s - 1) for s in edges]) for c in range(CHUNKS)]
    a0 = q0[0]
    dqs, dkvs, back_kv, dq1, dq2, parts = [], [], [], (), (), []
    diag = []
    for c in range(CHUNKS):
        diag.append(
            call(
                functools.partial(diag_kernel, c),
                [arr(WC, f32), arr(2 * WC, f32)],
                0,
                (q0[c], a0, kv, rank),
                flops=tile_flops // CHUNKS,
            )
        )
    q1[0], diag = lax.optimization_barrier((q1[0], diag))
    q2 = [shifted(q1[0], -2, lambda i: i % 2 == 1 and i % SPAN != SPAN - 1)]
    a1 = q1[0]
    for c in range(CHUNKS):
        dq, dkv = diag[c]
        dq, dkv, x, dkv1 = call(
            functools.partial(cross_kernel, c),
            [arr(WC, f32), arr(2 * WC, f32), arr((c + 1) * WC, bf16), arr(2 * WC, f32)],
            1,
            (odd, q0[c], a0, q1[c], a1, kv, k1, dq, dkv, *dq1),
            flops=3 * tile_flops // CHUNKS,
        )
        dq1 = (x,)
        dqs.append(dq)
        dkvs.append(dkv)
        parts.append(dkv1)
        if c == 0:
            q1[1], dq1 = lax.optimization_barrier((q1[1], dq1))
            q2.append(shifted(q1[1], -2, lambda i: i % 2 == 1 and i % SPAN != SPAN - 1))
    for c in range(CHUNKS):
        dkv1 = parts[c]
        x, send, q2[c] = call(
            functools.partial(last_kernel, c),
            [arr((c + 1) * WC, bf16), arr(2 * (c + 1) * WC, bf16), arr(qw[c], bf16)],
            1,
            (odd, q2[c], q2[0], k1, edge[c], dkv1, *dq2),
            flops=0,
            alias={1: 2},
        )
        dq2 = (x, send)
    x, send, dq1 = lax.optimization_barrier((x, send, dq1))
    r1 = swapped(dq1[0])
    r2 = lax.ppermute(x, AXES, [(i, i + 1) for i in range(1, n - 1, 2)])
    back = shifted(send, -2)
    (gq,) = call(sum_q, [arr(HEADS * SIZE, bf16)], 0, (*dqs, r1, r2), flops=20 << 30)
    gk, gv = call(sum_kv, [arr(HEADS * SIZE, bf16)] * 2, 0, (*dkvs, back), flops=1 << 20)
    return gq, gk, gv


def solution(mesh):
    rows = P(AXES, None)
    return jax.shard_map(
        per_device,
        mesh=mesh,
        in_specs=(rows, rows, rows, rows, rows, P(None, AXES), rows, rows),
        out_specs=(rows, rows, rows),
        check_vma=False,
    )
```

```python
import functools
import math

import jax
import jax.numpy as jnp
from jax import lax
from jax.experimental import pallas as pl
from jax.experimental.pallas import tpu as pltpu
from jax.sharding import PartitionSpec as P

AXES = ("inner", "outer")
HEADS = 8
SIZE = 64
PAIR = 2 * SIZE
CHUNKS = 2
COST = 8
SPAN = 128
HC = HEADS // CHUNKS
WC = HC * SIZE
EXP_SCALE = 0.125 / math.log(2.0)
HIDDEN = -1e30
f32 = jnp.float32
bf16 = jnp.bfloat16

VIS = 48


def dot(a, b, ca, cb):
    return lax.dot_general(a, b, (((ca,), (cb,)), ((), ())), preferred_element_type=f32)


def pieces(x):
    a = x.astype(bf16)
    r = x - a.astype(f32)
    b = r.astype(bf16)
    c = (r - b.astype(f32)).astype(bf16)
    return a, b, c


def pack_q(blk, layout, lse, order, everything, *outs):
    q, do, o = (everything.at[:, i * HEADS * SIZE : (i + 1) * HEADS * SIZE] for i in range(3))
    qs, rank = outs[:CHUNKS], outs[CHUNKS]
    rows = q.shape[0]
    for c in range(CHUNKS):
        w = slice(c * WC, (c + 1) * WC)
        qs[c][:, :WC] = q[:, w]
        qs[c][:, WC : 2 * WC] = do[:, w]
    lane = lax.broadcasted_iota(jnp.int32, (1, 128), 1)
    prod = do[...].astype(f32) * o[...].astype(f32)
    hi = prod.astype(bf16)
    lo = (prod - hi.astype(f32)).astype(bf16)
    feat = lax.broadcasted_iota(jnp.int32, (HEADS * SIZE, 128), 0) // SIZE
    flane = lax.broadcasted_iota(jnp.int32, (HEADS * SIZE, 128), 1)
    pick = jnp.where((flane % 8 == feat) & (flane >= 24) & (flane < 48), 1.0, 0.0).astype(bf16)
    delta = dot(hi, pick, 1, 0) + dot(lo, pick, 1, 0)
    d1, d2, d3 = (x.astype(f32) for x in pieces(delta))
    dpart = jnp.where(lane < 32, d1, jnp.where(lane < 40, d2, d3))
    l1, l2, l3 = (x.astype(f32) for x in pieces(lse[...] * 8.0))
    stack = jnp.concatenate([l1, l2, l3, jnp.zeros_like(l1)], 0).astype(bf16)
    r = lax.broadcasted_iota(jnp.int32, (32, 128), 0)
    c = lax.broadcasted_iota(jnp.int32, (32, 128), 1)
    eye = jnp.where((r == c) & (r < 24), 1.0, 0.0).astype(bf16)
    lpart = dot(stack, eye, 0, 0)
    vis = jnp.zeros((1, 128), f32)
    for d in (1, 2, 3):
        seen = jnp.logical_and(layout[0, d - 1] > 0, blk[0] >= d)
        vis = jnp.where((lane == VIS + d - 1) & jnp.logical_not(seen), f32(HIDDEN), vis)
    aux = jnp.where(lane < 24, lpart, jnp.where(lane < 48, dpart, jnp.broadcast_to(vis, (rows, 128))))
    qs[0][:, 2 * WC :] = aux.astype(bf16)
    rank[...] = jnp.broadcast_to(order[...].astype(f32), rank.shape)


def tile(q, aux, kv, c, hp, dist, rank_row=None, rank_col=None):
    at = pl.ds(pl.multiple_of(hp * PAIR, PAIR), PAIR)
    at2 = pl.ds(pl.multiple_of(WC + hp * PAIR, PAIR), PAIR)
    at_k = pl.ds(pl.multiple_of(c * WC + hp * PAIR, PAIR), PAIR)
    at_v = pl.ds(pl.multiple_of((CHUNKS + c) * WC + hp * PAIR, PAIR), PAIR)
    qp, dop, kp, vp = q[:, at], q[:, at2], kv[:, at_k], kv[:, at_v]
    lane = lax.broadcasted_iota(jnp.int32, (1, PAIR), 1)
    half = lax.broadcasted_iota(jnp.int32, qp.shape, 1) // SIZE
    qa = jnp.concatenate([qp, aux], 1)
    da = jnp.concatenate([dop, aux], 1)
    km, qm, dm, vm, sels, seld = [], [], [], [], [], []
    rows = qp.shape[0]
    for h in range(2):
        head = c * HC + hp * 2 + h
        sel = jnp.where((lane % 8 == head) & (lane < 24), -1.0, 0.0)
        if dist is not None:
            sel = jnp.where(lane == VIS - 1 + dist, 1.0, sel)
        sel_d = jnp.where((lane % 8 == head) & (lane >= 24) & (lane < 48), -1.0, 0.0)
        mine = half == h
        zero = jnp.zeros_like(kp)
        km.append(jnp.where(mine, kp, zero))
        vm.append(jnp.where(mine, vp, zero))
        qm.append(jnp.where(mine, qp, zero))
        dm.append(jnp.where(mine, dop, zero))
        sels.append(jnp.broadcast_to(sel, kp.shape).astype(bf16))
        seld.append(jnp.broadcast_to(sel_d, kp.shape).astype(bf16))
    k_both = jnp.concatenate(km, 0)
    s = dot(jnp.concatenate([k_both, jnp.concatenate(sels, 0)], 1), qa, 1, 1)
    dp = dot(jnp.concatenate([jnp.concatenate(vm, 0), jnp.concatenate(seld, 0)], 1), da, 1, 1)
    p = jnp.exp2(s * EXP_SCALE)
    if rank_row is not None:
        seen = rank_row >= rank_col
        p = jnp.where(jnp.concatenate([seen, seen], 0), p, 0.0)
    p_low, ds = p.astype(bf16), (p * dp).astype(bf16)
    pb, db = [p_low[:rows], p_low[rows:]], [ds[:rows], ds[rows:]]
    dv = dot(jnp.concatenate(pb, 1), jnp.concatenate(dm, 0), 1, 0)
    dk = dot(jnp.concatenate(db, 1), jnp.concatenate(qm, 0), 1, 0)
    dq = dot(k_both, ds, 0, 0).T
    return dq, dk, dv


def pairs(body):
    def step(hp, _):
        body(hp, pl.ds(pl.multiple_of(hp * PAIR, PAIR), PAIR), pl.ds(pl.multiple_of(WC + hp * PAIR, PAIR), PAIR))
        return 0

    lax.fori_loop(0, HC // 2, step, 0)


def diag_kernel(c, q, qa, kv, rank, dq, dkv):
    rank_col = jnp.broadcast_to(rank[:1], (128, rank.shape[1])).T[:, :1]

    def body(hp, at, at2):
        x, y, z = tile(q, qa[:, 2 * WC :], kv, c, hp, None, rank[:1], rank_col)
        dq[:, at] = x
        dkv[:, at] = y
        dkv[:, at2] = z

    pairs(body)


def cross_kernel(c, odd, q0, a0, q1, a1, k0, k1, dq, dkv, *refs):
    before, (dq_out, dkv_out, dq1, dkv1) = refs[:-4], refs[-4:]
    near = jnp.where(odd[0] & 1 == 0, 3, 1)

    base = 0
    for part in before:
        dq1[:, base : base + WC] = part[...]
        base += WC

    def body(hp, at, at2):
        x, y, z = tile(q0, a0[:, 2 * WC :], k1, c, hp, 2)
        dq_out[:, at] = dq[:, at] + x
        x, y2, z2 = tile(q1, a1[:, 2 * WC :], k1, c, hp, near)
        dkv1[:, at] = y + y2
        dkv1[:, at2] = z + z2
        to = pl.ds(pl.multiple_of(base + hp * PAIR, PAIR), PAIR)

        @pl.when(odd[0] & 1 == 0)
        def _():
            x3, y3, z3 = tile(q1, a1[:, 2 * WC :], k0, c, hp, 1)
            dq1[:, to] = ((x + x3) * 0.125).astype(bf16)
            dkv_out[:, at] = dkv[:, at] + y3
            dkv_out[:, at2] = dkv[:, at2] + z3

        @pl.when(odd[0] & 1 != 0)
        def _():
            dq1[:, to] = (x * 0.125).astype(bf16)
            dkv_out[:, at] = dkv[:, at]
            dkv_out[:, at2] = dkv[:, at2]

    pairs(body)


def last_kernel(c, odd, q2_far, a2_far, k1, edge, dkv1, *refs):
    before, (dq2, out, q2) = refs[:-3], refs[-3:]
    a2 = q2 if c == 0 else a2_far

    @pl.when(odd[0] & 8 != 0)
    def _():
        q2[...] = edge[...]


    base = 0
    for part in before:
        dq2[:, base : base + WC] = part[...]
        base += WC

    def body(hp, at, at2):
        to = pl.ds(pl.multiple_of(base + hp * PAIR, PAIR), PAIR)

        @pl.when(odd[0] & 1 != 0)
        def _():
            x, y, z = tile(q2, a2[:, 2 * WC :], k1, c, hp, 3)
            dq2[:, to] = (x * 0.125).astype(bf16)
            out[:, at] = ((dkv1[:, at] + y) * 0.125).astype(bf16)
            out[:, at2] = (dkv1[:, at2] + z).astype(bf16)

        @pl.when(odd[0] & 1 == 0)
        def _():
            dq2[:, to] = jnp.zeros((dq2.shape[0], PAIR), bf16)
            out[:, at] = (dkv1[:, at] * 0.125).astype(bf16)
            out[:, at2] = dkv1[:, at2].astype(bf16)

    pairs(body)


def first_sum(dq_a, dq_b, dkv, r1, r2, back, gq, gk, gv):
    far = r1[...].astype(f32) + r2[...].astype(f32)
    gq[:, :WC] = (dq_a[...] * 0.125 + far[:, :WC]).astype(bf16)
    gq[:, WC:] = (dq_b[...] * 0.125 + far[:, WC:]).astype(bf16)
    gk[...] = (dkv[:, :WC] * 0.125 + back[:, :WC].astype(f32)).astype(bf16)
    gv[...] = (dkv[:, WC:] + back[:, WC:].astype(f32)).astype(bf16)


def last_sum(pk, pv, dkv, back, gk, gv):
    gk[:, :WC] = pk[...]
    gv[:, :WC] = pv[...]
    gk[:, WC:] = (dkv[:, :WC] * 0.125 + back[:, :WC].astype(f32)).astype(bf16)
    gv[:, WC:] = (dkv[:, WC:] + back[:, WC:].astype(f32)).astype(bf16)


VM = pl.BlockSpec(memory_space=pltpu.VMEM)
SM = pl.BlockSpec(memory_space=pltpu.SMEM)


def call(kernel, outs, n_smem, args, scratch=(), flops=0, n_far=0, vmem=16, alias=None):
    near = len(args) - n_smem - n_far
    return pl.pallas_call(
        kernel,
        out_shape=outs,
        in_specs=[SM] * n_smem + [VM] * near + [pl.BlockSpec(memory_space=pltpu.HBM)] * n_far,
        out_specs=[VM] * len(outs),
        scratch_shapes=list(scratch),
        input_output_aliases=alias or {},
        cost_estimate=pl.CostEstimate(flops=flops, bytes_accessed=1 << 10, transcendentals=0),
        compiler_params=pltpu.CompilerParams(vmem_limit_bytes=vmem << 20),
    )(*args)


def per_device(query, keys, values, output, grad_output, log_sum_exp, order, layout):
    rows = query.shape[0]
    n = lax.axis_size(AXES)
    block = lax.axis_index(AXES)
    blk = jnp.reshape(block, (1,)).astype(jnp.int32)
    parity, place = block % 2, block % SPAN
    takes = jnp.where((place == SPAN - 1) & (block < n - 1), 8, 0)
    odd = jnp.reshape(parity + takes, (1,)).astype(jnp.int32)
    edges = range(SPAN, n, SPAN)

    def arr(cols, kind):
        return jax.ShapeDtypeStruct((rows, cols), kind)

    def shifted(x, by, keep=lambda i: True):
        return lax.ppermute(x, AXES, [(i - by, i) for i in range(n) if 0 <= i - by < n and keep(i)])

    def swapped(x):
        return lax.ppermute(x, AXES, [(i ^ 1, i) for i in range(n)])

    tile_flops = COST * 5 * 2 * rows * rows * SIZE * HEADS
    qw = [2 * WC + (128 if c == 0 else 0) for c in range(CHUNKS)]
    kv = jnp.concatenate([keys, values], 1)
    k1 = shifted(kv, 2)
    kv, query = lax.optimization_barrier((kv, query))
    *q0, rank = call(
        pack_q,
        [arr(w, bf16) for w in qw] + [jax.ShapeDtypeStruct((8, rows), f32)],
        2,
        (blk, layout, log_sum_exp, order, jnp.concatenate([query, grad_output, output], 1)),
    )
    q1 = [swapped(q0[c]) for c in range(CHUNKS)]
    edge = [lax.ppermute(q0[c], AXES, [(s, s - 1) for s in edges]) for c in range(CHUNKS)]
    a0 = q0[0]
    dqs, dkvs, back_kv, dq1, dq2, parts = [], [], [], (), (), []
    diag = []
    for c in range(CHUNKS):
        diag.append(
            call(
                functools.partial(diag_kernel, c),
                [arr(WC, f32), arr(2 * WC, f32)],
                0,
                (q0[c], a0, kv, rank),
                flops=tile_flops // CHUNKS,
            )
        )
    q1[0], diag = lax.optimization_barrier((q1[0], diag))
    q2 = [shifted(q1[0], -2, lambda i: i % 2 == 1 and i % SPAN != SPAN - 1)]
    a1 = q1[0]
    for c in range(CHUNKS):
        dq, dkv = diag[c]
        dq, dkv, x, dkv1 = call(
            functools.partial(cross_kernel, c),
            [arr(WC, f32), arr(2 * WC, f32), arr((c + 1) * WC, bf16), arr(2 * WC, f32)],
            1,
            (odd, q0[c], a0, q1[c], a1, kv, k1, dq, dkv, *dq1),
            flops=3 * tile_flops // CHUNKS,
        )
        dq1 = (x,)
        dqs.append(dq)
        dkvs.append(dkv)
        parts.append(dkv1)
        if c == 0:
            q1[1], dq1 = lax.optimization_barrier((q1[1], dq1))
            q2.append(shifted(q1[1], -2, lambda i: i % 2 == 1 and i % SPAN != SPAN - 1))
    for c in range(CHUNKS):
        dkv1 = parts[c]
        x, send, q2[c] = call(
            functools.partial(last_kernel, c),
            [arr((c + 1) * WC, bf16), arr(2 * WC, bf16), arr(qw[c], bf16)],
            1,
            (odd, q2[c], q2[0], k1, edge[c], dkv1, *dq2),
            flops=0,
            alias={1: 2},
        )
        dq2 = (x,)
        if c == 0:
            dq1, dq2 = lax.optimization_barrier((dq1, dq2))
            back_q1 = swapped(dq1[0])
        back_kv.append(shifted(send, -2))
    back_q2 = lax.ppermute(dq2[0], AXES, [(i, i + 1) for i in range(1, n - 1, 2)])
    gq, pk, pv = call(
        first_sum,
        [arr(HEADS * SIZE, bf16), arr(WC, bf16), arr(WC, bf16)],
        0,
        (*dqs, dkvs[0], back_q1, back_q2, back_kv[0]),
        flops=20 << 30,
    )
    gk, gv = call(last_sum, [arr(HEADS * SIZE, bf16)] * 2, 0, (pk, pv, dkvs[1], back_kv[1]), flops=1 << 20)
    return gq, gk, gv


def solution(mesh):
    rows = P(AXES, None)
    return jax.shard_map(
        per_device,
        mesh=mesh,
        in_specs=(rows, rows, rows, rows, rows, P(None, AXES), rows, rows),
        out_specs=(rows, rows, rows),
        check_vma=False,
    )
```

```python
import functools
import math

import jax
import jax.numpy as jnp
from jax import lax
from jax.experimental import pallas as pl
from jax.experimental.pallas import tpu as pltpu
from jax.sharding import PartitionSpec as P

AXES = ("inner", "outer")
HEADS = 8
SIZE = 64
PAIR = 2 * SIZE
CHUNKS = 2
COST = 8
SPAN = 128
HC = HEADS // CHUNKS
WC = HC * SIZE
EXP_SCALE = 0.125 / math.log(2.0)
HIDDEN = -1e30
f32 = jnp.float32
bf16 = jnp.bfloat16

VIS = 48


def dot(a, b, ca, cb):
    return lax.dot_general(a, b, (((ca,), (cb,)), ((), ())), preferred_element_type=f32)


def pieces(x):
    a = x.astype(bf16)
    r = x - a.astype(f32)
    b = r.astype(bf16)
    c = (r - b.astype(f32)).astype(bf16)
    return a, b, c


def pack_q(blk, layout, lse, order, everything, *outs):
    q, do, o = (everything.at[:, i * HEADS * SIZE : (i + 1) * HEADS * SIZE] for i in range(3))
    qs, rank = outs[:CHUNKS], outs[CHUNKS]
    rows = q.shape[0]
    for c in range(CHUNKS):
        w = slice(c * WC, (c + 1) * WC)
        qs[c][:, :WC] = q[:, w]
        qs[c][:, WC : 2 * WC] = do[:, w]
    lane = lax.broadcasted_iota(jnp.int32, (1, 128), 1)
    prod = do[...].astype(f32) * o[...].astype(f32)
    hi = prod.astype(bf16)
    lo = (prod - hi.astype(f32)).astype(bf16)
    feat = lax.broadcasted_iota(jnp.int32, (HEADS * SIZE, 128), 0) // SIZE
    flane = lax.broadcasted_iota(jnp.int32, (HEADS * SIZE, 128), 1)
    pick = jnp.where((flane % 8 == feat) & (flane >= 24) & (flane < 48), 1.0, 0.0).astype(bf16)
    delta = dot(hi, pick, 1, 0) + dot(lo, pick, 1, 0)
    d1, d2, d3 = (x.astype(f32) for x in pieces(delta))
    dpart = jnp.where(lane < 32, d1, jnp.where(lane < 40, d2, d3))
    l1, l2, l3 = (x.astype(f32) for x in pieces(lse[...] * 8.0))
    stack = jnp.concatenate([l1, l2, l3, jnp.zeros_like(l1)], 0).astype(bf16)
    r = lax.broadcasted_iota(jnp.int32, (32, 128), 0)
    c = lax.broadcasted_iota(jnp.int32, (32, 128), 1)
    eye = jnp.where((r == c) & (r < 24), 1.0, 0.0).astype(bf16)
    lpart = dot(stack, eye, 0, 0)
    vis = jnp.zeros((1, 128), f32)
    for d in (1, 2, 3):
        seen = jnp.logical_and(layout[0, d - 1] > 0, blk[0] >= d)
        vis = jnp.where((lane == VIS + d - 1) & jnp.logical_not(seen), f32(HIDDEN), vis)
    aux = jnp.where(lane < 24, lpart, jnp.where(lane < 48, dpart, jnp.broadcast_to(vis, (rows, 128))))
    qs[0][:, 2 * WC :] = aux.astype(bf16)
    rank[...] = jnp.broadcast_to(order[...].astype(f32), rank.shape)


def tile(q, aux, kv, c, hp, dist, rank_row=None, rank_col=None):
    at = pl.ds(pl.multiple_of(hp * PAIR, PAIR), PAIR)
    at2 = pl.ds(pl.multiple_of(WC + hp * PAIR, PAIR), PAIR)
    at_k = pl.ds(pl.multiple_of(c * WC + hp * PAIR, PAIR), PAIR)
    at_v = pl.ds(pl.multiple_of((CHUNKS + c) * WC + hp * PAIR, PAIR), PAIR)
    qp, dop, kp, vp = q[:, at], q[:, at2], kv[:, at_k], kv[:, at_v]
    lane = lax.broadcasted_iota(jnp.int32, (1, PAIR), 1)
    half = lax.broadcasted_iota(jnp.int32, qp.shape, 1) // SIZE
    qa = jnp.concatenate([qp, aux], 1)
    da = jnp.concatenate([dop, aux], 1)
    km, qm, dm, vm, sels, seld = [], [], [], [], [], []
    rows = qp.shape[0]
    for h in range(2):
        head = c * HC + hp * 2 + h
        sel = jnp.where((lane % 8 == head) & (lane < 24), -1.0, 0.0)
        if dist is not None:
            sel = jnp.where(lane == VIS - 1 + dist, 1.0, sel)
        sel_d = jnp.where((lane % 8 == head) & (lane >= 24) & (lane < 48), -1.0, 0.0)
        mine = half == h
        zero = jnp.zeros_like(kp)
        km.append(jnp.where(mine, kp, zero))
        vm.append(jnp.where(mine, vp, zero))
        qm.append(jnp.where(mine, qp, zero))
        dm.append(jnp.where(mine, dop, zero))
        sels.append(jnp.broadcast_to(sel, kp.shape).astype(bf16))
        seld.append(jnp.broadcast_to(sel_d, kp.shape).astype(bf16))
    k_both = jnp.concatenate(km, 0)
    s = dot(jnp.concatenate([k_both, jnp.concatenate(sels, 0)], 1), qa, 1, 1)
    dp = dot(jnp.concatenate([jnp.concatenate(vm, 0), jnp.concatenate(seld, 0)], 1), da, 1, 1)
    p = jnp.exp2(s * EXP_SCALE)
    if rank_row is not None:
        seen = rank_row >= rank_col
        p = jnp.where(jnp.concatenate([seen, seen], 0), p, 0.0)
    p_low, ds = p.astype(bf16), (p * dp).astype(bf16)
    pb, db = [p_low[:rows], p_low[rows:]], [ds[:rows], ds[rows:]]
    dv = dot(jnp.concatenate(pb, 1), jnp.concatenate(dm, 0), 1, 0)
    dk = dot(jnp.concatenate(db, 1), jnp.concatenate(qm, 0), 1, 0)
    dq = dot(k_both, ds, 0, 0).T
    return dq, dk, dv


def pairs(body):
    def step(hp, _):
        body(hp, pl.ds(pl.multiple_of(hp * PAIR, PAIR), PAIR), pl.ds(pl.multiple_of(WC + hp * PAIR, PAIR), PAIR))
        return 0

    lax.fori_loop(0, HC // 2, step, 0)


def diag_kernel(c, q, qa, kv, rank, dq, dkv):
    rank_col = jnp.broadcast_to(rank[:1], (128, rank.shape[1])).T[:, :1]

    def body(hp, at, at2):
        x, y, z = tile(q, qa[:, 2 * WC :], kv, c, hp, None, rank[:1], rank_col)
        dq[:, at] = x
        dkv[:, at] = y
        dkv[:, at2] = z

    pairs(body)


def cross_kernel(c, odd, q0, a0, q1, a1, k0, k1, dq, dkv, *refs):
    before, (dq_out, dkv_out, dq1, dkv1) = refs[:-4], refs[-4:]
    near = jnp.where(odd[0] & 1 == 0, 3, 1)

    base = 0
    for part in before:
        dq1[:, base : base + WC] = part[...]
        base += WC

    def body(hp, at, at2):
        x, y, z = tile(q0, a0[:, 2 * WC :], k1, c, hp, 2)
        dq_out[:, at] = dq[:, at] + x
        x, y2, z2 = tile(q1, a1[:, 2 * WC :], k1, c, hp, near)
        dkv1[:, at] = y + y2
        dkv1[:, at2] = z + z2
        to = pl.ds(pl.multiple_of(base + hp * PAIR, PAIR), PAIR)

        @pl.when(odd[0] & 1 == 0)
        def _():
            x3, y3, z3 = tile(q1, a1[:, 2 * WC :], k0, c, hp, 1)
            dq1[:, to] = ((x + x3) * 0.125).astype(bf16)
            dkv_out[:, at] = dkv[:, at] + y3
            dkv_out[:, at2] = dkv[:, at2] + z3

        @pl.when(odd[0] & 1 != 0)
        def _():
            dq1[:, to] = (x * 0.125).astype(bf16)
            dkv_out[:, at] = dkv[:, at]
            dkv_out[:, at2] = dkv[:, at2]

    pairs(body)


def last_kernel(c, odd, q2_far, a2_far, k1, edge, dkv1, *refs):
    before, (dq2, out, q2) = refs[:-3], refs[-3:]
    a2 = q2 if c == 0 else a2_far

    @pl.when(odd[0] & 8 != 0)
    def _():
        q2[...] = edge[...]


    base = 0
    for part in before:
        dq2[:, base : base + WC] = part[...]
        base += WC

    def body(hp, at, at2):
        to = pl.ds(pl.multiple_of(base + hp * PAIR, PAIR), PAIR)

        @pl.when(odd[0] & 1 != 0)
        def _():
            x, y, z = tile(q2, a2[:, 2 * WC :], k1, c, hp, 3)
            dq2[:, to] = (x * 0.125).astype(bf16)
            out[:, at] = ((dkv1[:, at] + y) * 0.125).astype(bf16)
            out[:, at2] = (dkv1[:, at2] + z).astype(bf16)

        @pl.when(odd[0] & 1 == 0)
        def _():
            dq2[:, to] = jnp.zeros((dq2.shape[0], PAIR), bf16)
            out[:, at] = (dkv1[:, at] * 0.125).astype(bf16)
            out[:, at2] = dkv1[:, at2].astype(bf16)

    pairs(body)


def first_sum(dq_a, dq_b, dkv, r1, back, gq, gk, gv):
    gq[:, :WC] = dq_a[...] * 0.125 + r1[:, :WC].astype(f32)
    gq[:, WC:] = dq_b[...] * 0.125 + r1[:, WC:].astype(f32)
    gk[...] = (dkv[:, :WC] * 0.125 + back[:, :WC].astype(f32)).astype(bf16)
    gv[...] = (dkv[:, WC:] + back[:, WC:].astype(f32)).astype(bf16)


def last_sum(pq, pk, pv, dkv, r2, back, gq, gk, gv):
    gq[...] = (pq[...] + r2[...].astype(f32)).astype(bf16)
    gk[:, :WC] = pk[...]
    gv[:, :WC] = pv[...]
    gk[:, WC:] = (dkv[:, :WC] * 0.125 + back[:, :WC].astype(f32)).astype(bf16)
    gv[:, WC:] = (dkv[:, WC:] + back[:, WC:].astype(f32)).astype(bf16)


VM = pl.BlockSpec(memory_space=pltpu.VMEM)
SM = pl.BlockSpec(memory_space=pltpu.SMEM)


def call(kernel, outs, n_smem, args, scratch=(), flops=0, n_far=0, vmem=16, alias=None):
    near = len(args) - n_smem - n_far
    return pl.pallas_call(
        kernel,
        out_shape=outs,
        in_specs=[SM] * n_smem + [VM] * near + [pl.BlockSpec(memory_space=pltpu.HBM)] * n_far,
        out_specs=[VM] * len(outs),
        scratch_shapes=list(scratch),
        input_output_aliases=alias or {},
        cost_estimate=pl.CostEstimate(flops=flops, bytes_accessed=1 << 10, transcendentals=0),
        compiler_params=pltpu.CompilerParams(vmem_limit_bytes=vmem << 20),
    )(*args)


def per_device(query, keys, values, output, grad_output, log_sum_exp, order, layout):
    rows = query.shape[0]
    n = lax.axis_size(AXES)
    block = lax.axis_index(AXES)
    blk = jnp.reshape(block, (1,)).astype(jnp.int32)
    parity, place = block % 2, block % SPAN
    takes = jnp.where((place == SPAN - 1) & (block < n - 1), 8, 0)
    odd = jnp.reshape(parity + takes, (1,)).astype(jnp.int32)
    edges = range(SPAN, n, SPAN)

    def arr(cols, kind):
        return jax.ShapeDtypeStruct((rows, cols), kind)

    def shifted(x, by, keep=lambda i: True):
        return lax.ppermute(x, AXES, [(i - by, i) for i in range(n) if 0 <= i - by < n and keep(i)])

    def swapped(x):
        return lax.ppermute(x, AXES, [(i ^ 1, i) for i in range(n)])

    tile_flops = COST * 5 * 2 * rows * rows * SIZE * HEADS
    qw = [2 * WC + (128 if c == 0 else 0) for c in range(CHUNKS)]
    kv = jnp.concatenate([keys, values], 1)
    k1 = shifted(kv, 2)
    kv, query = lax.optimization_barrier((kv, query))
    *q0, rank = call(
        pack_q,
        [arr(w, bf16) for w in qw] + [jax.ShapeDtypeStruct((8, rows), f32)],
        2,
        (blk, layout, log_sum_exp, order, jnp.concatenate([query, grad_output, output], 1)),
    )
    q1 = [swapped(q0[c]) for c in range(CHUNKS)]
    edge = [lax.ppermute(q0[c], AXES, [(s, s - 1) for s in edges]) for c in range(CHUNKS)]
    a0 = q0[0]
    dqs, dkvs, back_kv, dq1, dq2, parts = [], [], [], (), (), []
    diag = []
    for c in range(CHUNKS):
        diag.append(
            call(
                functools.partial(diag_kernel, c),
                [arr(WC, f32), arr(2 * WC, f32)],
                0,
                (q0[c], a0, kv, rank),
                flops=tile_flops // CHUNKS,
            )
        )
    q1[0], diag = lax.optimization_barrier((q1[0], diag))
    q2 = [shifted(q1[0], -2, lambda i: i % 2 == 1 and i % SPAN != SPAN - 1)]
    a1 = q1[0]
    for c in range(CHUNKS):
        dq, dkv = diag[c]
        dq, dkv, x, dkv1 = call(
            functools.partial(cross_kernel, c),
            [arr(WC, f32), arr(2 * WC, f32), arr((c + 1) * WC, bf16), arr(2 * WC, f32)],
            1,
            (odd, q0[c], a0, q1[c], a1, kv, k1, dq, dkv, *dq1),
            flops=3 * tile_flops // CHUNKS,
        )
        dq1 = (x,)
        dqs.append(dq)
        dkvs.append(dkv)
        parts.append(dkv1)
        if c == 0:
            q1[1], dq1 = lax.optimization_barrier((q1[1], dq1))
            q2.append(shifted(q1[1], -2, lambda i: i % 2 == 1 and i % SPAN != SPAN - 1))
    for c in range(CHUNKS):
        dkv1 = parts[c]
        x, send, q2[c] = call(
            functools.partial(last_kernel, c),
            [arr((c + 1) * WC, bf16), arr(2 * WC, bf16), arr(qw[c], bf16)],
            1,
            (odd, q2[c], q2[0], k1, edge[c], dkv1, *dq2),
            flops=0,
            alias={1: 2},
        )
        dq2 = (x,)
        if c == 0:
            dq1, dq2 = lax.optimization_barrier((dq1, dq2))
            back_q1 = swapped(dq1[0])
        back_kv.append(shifted(send, -2))
    back_q2 = lax.ppermute(dq2[0], AXES, [(i, i + 1) for i in range(1, n - 1, 2)])
    part = call(
        first_sum,
        [arr(HEADS * SIZE, f32), arr(WC, bf16), arr(WC, bf16)],
        0,
        (*dqs, dkvs[0], back_q1, back_kv[0]),
        flops=20 << 30,
    )
    return tuple(
        call(last_sum, [arr(HEADS * SIZE, bf16)] * 3, 0, (*part, dkvs[1], back_q2, back_kv[1]), flops=1 << 20)
    )


def solution(mesh):
    rows = P(AXES, None)
    return jax.shard_map(
        per_device,
        mesh=mesh,
        in_specs=(rows, rows, rows, rows, rows, P(None, AXES), rows, rows),
        out_specs=(rows, rows, rows),
        check_vma=False,
    )
```
